128 devices in a mesh: row: 16 (over x, z_lo, core), col: 8 (over z_hi, y).
Axes of the slice: x: 4, y: 4, z: 4 (z_hi: 2, z_lo: 2; z = z_hi * 2 + z_lo), core: 2. Of those that a mesh axis runs over, the one named last changes fastest.
Arguments:
- lambda_tiles: bfloat16 [96, 2048, 2048], P('row', 'col'), may hold values from -6 to 6
- dressing: bfloat16 [2048, 2048], P(('row', 'col')), may hold values from -0.125 to 0.125
- constant_term: bfloat16 [96, 2048, 2048], P('row', 'col'), may hold values from -6 to 6
- domain_mask: int32 [96, 32], P('row'), may hold values from 0 to 1, as said below
- virtual_energy: float32 [2048], replicated, may hold values from 0.2 to 1
- pair_shift: float32 [96], P('row'), may hold values from 0.1 to 1
Outputs:
- lambda_next: bfloat16 [96, 2048, 2048], P('row', 'col')
The draws below stay inside these ranges and needn't reach their ends.
Inputs may be any that keep to these rules, and one draw needn't show every extreme that they name: `domain_mask`: each pair's domain is a nonempty subset of the 32 tiles; sizes differ from pair to pair.
All inputs are finite; a program needn't handle non-finite values.
Results may differ from the reference program's by a relative error of at most 0.001.
Values may be sent and summed in bfloat16 or wider, within the bound.
A program may use at most 128 MiB of HBM per device.

```python
import math
import jax
import jax.numpy as jnp
from jax import lax

V = 2048
TILE = 64
VT = 32
NPAIR = 96


def draw_domain_mask(key, part):
    key = jax.random.fold_in(key, 7)
    first_key, second_key = jax.random.split(key)
    domain_size = jax.random.randint(first_key, (NPAIR, 1), 1, VT + 1)
    scores = jax.random.randint(second_key, (NPAIR, VT), 0, VT)
    pair_index = jnp.arange(NPAIR, dtype=jnp.int32)[:, None] % VT
    tile_index = jnp.arange(VT, dtype=jnp.int32)[None, :]
    chosen = jnp.logical_or(scores < domain_size, tile_index == pair_index)
    return chosen.astype(jnp.int32)


def level_of(rng, extent, shards, smallest, high):
    factor_of, own = 1.0, jax.random.fold_in(rng, 6)
    for axis_at, parts in shards:
        heights = jnp.exp(jax.random.uniform(jax.random.fold_in(own, axis_at), (parts,), jnp.float32, smallest / len(shards), high / len(shards)))
        factor_of = factor_of * jnp.repeat(heights, extent[axis_at] // parts).reshape([-1 if axis == axis_at else 1 for axis in range(len(extent))])
    return factor_of


def normal_values(stream_key, extent, scale, limit, cuts=(), kind=jnp.bfloat16):
    factor_of = level_of(stream_key, extent, cuts, -0.22, 0.18) if cuts else 1.0
    entries = jax.random.normal(stream_key, extent, jnp.float32) * scale * factor_of
    return jnp.minimum(jnp.maximum(entries, -limit), limit).astype(kind)


def setup_inputs(seed: int = 0) -> dict:
    keys = jax.random.split(jax.random.key(seed), 7)
    return {
        "lambda_tiles": normal_values(keys[0], (NPAIR, V, V), 1.0, 6.0, ((0, 16), (1, 8))),
        "dressing": normal_values(keys[1], (V, V), V ** -0.5, 0.125, ((0, 128),)),
        "constant_term": normal_values(keys[2], (NPAIR, V, V), 1.0, 6.0, ((0, 16), (1, 8))),
        "domain_mask": draw_domain_mask(jax.random.fold_in(keys[6], 71), 0),
        "virtual_energy": jnp.clip(jax.random.uniform(keys[4], (V,), jnp.float32, 0.2, 1.0), 0.2, 1.0),
        "pair_shift": jnp.clip(jnp.exp(math.log(1.0) - 2.3025851 * jax.random.uniform(keys[5], (NPAIR,), jnp.float32) ** level_of(keys[5], (NPAIR,), ((0, 16),), -0.2, 0.2)), 0.1, 1.0),
    }


def reference(lambda_tiles, dressing, constant_term, domain_mask, virtual_energy, pair_shift):
    tile_mask = jnp.repeat(domain_mask.astype(jnp.float32), TILE, axis=1)

    def one_pair(index):
        amplitude = lambda_tiles[index]
        vector_mask = tile_mask[index]
        domain = vector_mask[:, None] * vector_mask[None, :]
        masked = jnp.where(domain > 0, amplitude, jnp.zeros_like(amplitude))
        product = jnp.dot(masked, dressing, preferred_element_type=jnp.float32)
        residual = domain * (constant_term[index].astype(jnp.float32) + product)
        return (masked, residual)
    masked, residual = lax.map(one_pair, jnp.arange(NPAIR, dtype=jnp.int32))
    squares = jnp.sum(residual * residual)
    factor = 0.25 * lax.rsqrt(squares / (NPAIR * V * V) + 1e-06)
    denominator = virtual_energy[None, :, None] + virtual_energy[None, None, :] + pair_shift[:, None, None]
    return (masked.astype(jnp.float32) + factor * residual / denominator).astype(jnp.bfloat16)
```

```python
import jax
import jax.numpy as jnp
from jax import lax
from jax.experimental import pallas as pl
from jax.experimental.pallas import tpu as pltpu
from jax.sharding import PartitionSpec as P

MESH = pl.DeviceIdType.MESH
F32, BF16 = jnp.float32, jnp.bfloat16
TILE = 64
PAIRS, ROWS, V = 6, 256, 2048
WIDTH = 256
STRIPS = V // WIDTH
DEVICES = 128
ENTRIES = 96 * V * V
ORDERS = ("yzx", "xyz", "zxy")
HOPS = (2, 1, 3)
MTILE = 768


def place():
    row, col = lax.axis_index("row"), lax.axis_index("col")
    return {
        "x": row // 4,
        "zl": (row // 2) % 2,
        "c": row % 2,
        "zh": col // 4,
        "y": col % 4,
        "z": (col // 4) * 2 + (row // 2) % 2,
    }


def device(at):
    return {"row": at["x"] * 4 + (at["z"] % 2) * 2 + at["c"], "col": (at["z"] // 2) * 4 + at["y"]}


def neighbour(at, axis, hops):
    moved = dict(at)
    moved[axis] = (at[axis] + hops) % 4
    return device(moved)


def sibling(at):
    moved = dict(at)
    moved["c"] = 1 - at["c"]
    return device(moved)


def block(gathered, strip, at, whole):
    every = slice(None)
    return gathered.at[
        strip,
        every if "x" in whole else at["x"],
        every if "z" in whole else at["zl"],
        at["c"],
        every if "z" in whole else at["zh"],
        every if "y" in whole else at["y"],
    ]


def gather_kernel(
    lam_hbm, dress_hbm, const_hbm, mask_ref, energy_ref, shift_ref,
    resid_ref, masked_ref, factor_ref,
    gathered, const_ref, colmask, rowmask, squares, mine, everyone,
    load_sem, own_sem, send_sem, recv_sem, sib_send, sib_recv, sum_send, sum_recv,
):
    at = place()
    barrier = pltpu.get_barrier_semaphore()
    partners = [neighbour(at, axis, hops) for axis in "xyz" for hops in HOPS] + [sibling(at)]
    for partner in partners:
        pl.semaphore_signal(barrier, inc=1, device_id=partner, device_id_type=MESH)

    own = [
        pltpu.make_async_copy(
            dress_hbm.at[:, pl.ds(s * WIDTH, WIDTH)], block(gathered, s, at, ""), own_sem.at[s]
        )
        for s in range(STRIPS)
    ]
    for copy in own:
        copy.start()
    loads = []
    for p in range(PAIRS):
        rows = pl.ds(p * ROWS, ROWS)
        loads.append(pltpu.make_async_copy(lam_hbm.at[p], masked_ref.at[rows, :], load_sem.at[0, p]))
        loads.append(pltpu.make_async_copy(const_hbm.at[p], const_ref.at[rows, :], load_sem.at[1, p]))
    for copy in loads:
        copy.start()
    for copy in own:
        copy.wait()
    pl.semaphore_wait(barrier, len(partners))

    def spread(phase, s):
        order = ORDERS[s % 3]
        part = block(gathered, s, at, order[:phase])
        return [
            pltpu.make_async_remote_copy(
                src_ref=part,
                dst_ref=part,
                send_sem=send_sem.at[phase, s, k],
                recv_sem=recv_sem.at[phase, s, k],
                device_id=neighbour(at, order[phase], hops),
                device_id_type=MESH,
            )
            for k, hops in enumerate(HOPS)
        ]

    sent = []

    def start(copies):
        for copy in copies:
            copy.start()
        sent.extend(copies)
        return copies

    first = [start(spread(0, s)) for s in range(STRIPS)]

    mask = mask_ref[...].astype(F32)
    tile_of = lax.broadcasted_iota(jnp.int32, (VT, V), 0)
    tile_col = lax.broadcasted_iota(jnp.int32, (VT, V), 1) // TILE
    cols_of = jnp.dot(mask, (tile_of == tile_col).astype(F32), preferred_element_type=F32)
    col = lax.axis_index("col")
    row_tile = lax.broadcasted_iota(jnp.int32, (ROWS, VT), 0) // TILE + col * (ROWS // TILE)
    row_hot = (row_tile == lax.broadcasted_iota(jnp.int32, (ROWS, VT), 1)).astype(F32)
    for p in range(PAIRS):
        colmask[p] = cols_of[p : p + 1, :]
        rowmask[p] = jnp.sum(row_hot * mask[p : p + 1, :], axis=1, keepdims=True)

    def prepare(pairs):
        for p in pairs:
            rows = pl.ds(p * ROWS, ROWS)
            loads[2 * p].wait()
            loads[2 * p + 1].wait()
            domain = (rowmask[p] * colmask[p]).astype(BF16)
            masked_ref[rows, :] = masked_ref[rows, :] * domain
            const_ref[rows, :] = const_ref[rows, :] * domain

    second, third = [], []
    for s in range(STRIPS):
        for copy in first[s]:
            copy.wait_recv()
        second.append(start(spread(1, s)))
    prepare(range(PAIRS))
    for s in range(STRIPS):
        for copy in second[s]:
            copy.wait_recv()
        third.append(start(spread(2, s)))

    def hand_over(s):
        part = block(gathered, s, at, "xyz")
        return pltpu.make_async_remote_copy(
            src_ref=part,
            dst_ref=part,
            send_sem=sib_send.at[s],
            recv_sem=sib_recv.at[s],
            device_id=sibling(at),
            device_id_type=MESH,
        )

    across = []

    def land(s):
        for copy in third[s]:
            copy.wait_recv()
        across.append(hand_over(s))
        across[s].start()

    squares[...] = jnp.zeros_like(squares)

    def multiply(s):
        cols = pl.ds(s * WIDTH, WIDTH)

        def tile(i, carry):
            rows = pl.ds(pl.multiple_of(i * MTILE, MTILE), MTILE)
            strip = gathered[s].reshape(V, WIDTH)
            product = jnp.dot(masked_ref[rows, :], strip, preferred_element_type=F32)
            total = jnp.zeros((8, WIDTH), F32)
            for q in range(MTILE // ROWS):
                pair_rows = pl.ds(pl.multiple_of(i * MTILE + q * ROWS, ROWS), ROWS)
                inside = colmask[i * (MTILE // ROWS) + q, :, cols]
                part = const_ref[pair_rows, cols].astype(F32) + inside * product[q * ROWS : (q + 1) * ROWS, :]
                resid_ref[pair_rows, cols] = part
                total = total + jnp.sum((part * part).reshape(ROWS // 8, 8, WIDTH), axis=0)
            squares[...] += total
            return carry

        lax.fori_loop(0, PAIRS * ROWS // MTILE, tile, 0)

    land(0)
    for s in range(STRIPS):
        if s + 1 < STRIPS:
            land(s + 1)
        across[s].wait_recv()
        multiply(s)

    eight = squares[:, :128] + squares[:, 128:]
    mine[...] = jnp.sum(eight, axis=0, keepdims=True)
    me = lax.axis_index("row") * 8 + col
    sums = []
    for step in range(1, DEVICES):
        other = (me + step) % DEVICES
        sums.append(
            pltpu.make_async_remote_copy(
                src_ref=mine,
                dst_ref=everyone.at[me],
                send_sem=sum_send.at[step],
                recv_sem=sum_recv.at[step],
                device_id={"row": other // 8, "col": other % 8},
                device_id_type=MESH,
            )
        )
    for copy in sums:
        copy.start()
    everyone[me] = mine[...]

    start_col = pl.multiple_of(col * ROWS, ROWS)
    own_energy = energy_ref[:, pl.ds(start_col, ROWS)]
    diagonal = lax.broadcasted_iota(jnp.int32, (ROWS, ROWS), 0) == lax.broadcasted_iota(jnp.int32, (ROWS, ROWS), 1)
    energy_rows = jnp.sum(jnp.where(diagonal, own_energy, 0.0), axis=1, keepdims=True)

    for p in range(PAIRS):
        shifted = energy_rows + shift_ref[p]
        for s in range(STRIPS):
            rows, cols = pl.ds(p * ROWS, ROWS), pl.ds(s * WIDTH, WIDTH)
            resid_ref[rows, cols] = resid_ref[rows, cols] / (shifted + energy_ref[:, cols])

    for copy in sums:
        copy.wait_recv()
    total = jnp.sum(jnp.sum(everyone[...], axis=0), axis=1, keepdims=True)
    factor = 0.25 * lax.rsqrt(total / ENTRIES + 1e-06)
    factor_ref[...] = jnp.zeros((8, 128), F32) + factor

    for copy in sent + across + sums:
        copy.wait_send()


VT = V // TILE
CHUNK = 128


def update_kernel(resid_ref, masked_ref, factor_ref, out_hbm, staged, sem):
    factor = factor_ref[0:1, 0:1]
    copies = []
    for i in range(PAIRS * ROWS // CHUNK):
        rows = pl.ds(i * CHUNK, CHUNK)
        staged[rows, :] = (masked_ref[rows, :].astype(F32) + factor * resid_ref[rows, :]).astype(BF16)
        copies.append(pltpu.make_async_copy(staged.at[rows, :], out_hbm.at[rows, :], sem.at[i]))
        copies[-1].start()
    for copy in copies:
        copy.wait()


def per_device(lambda_tiles, dressing, constant_term, domain_mask, virtual_energy, pair_shift):
    vmem, hbm, smem = (pl.BlockSpec(memory_space=m) for m in (pltpu.VMEM, pl.ANY, pltpu.SMEM))
    flat = (PAIRS * ROWS, V)
    dma = pltpu.SemaphoreType.DMA
    resid, masked, factor = pl.pallas_call(
        gather_kernel,
        name="gather_multiply",
        out_shape=(pltpu.VMEM(flat, F32), pltpu.VMEM(flat, BF16), pltpu.VMEM((8, 128), F32)),
        in_specs=[hbm, hbm, hbm, vmem, vmem, smem],
        out_specs=(vmem, vmem, vmem),
        scratch_shapes=[
            pltpu.VMEM((STRIPS, 4, 2, 2, 2, 4, 16, WIDTH), BF16),
            pltpu.VMEM(flat, BF16),
            pltpu.VMEM((PAIRS, 1, V), F32),
            pltpu.VMEM((PAIRS, ROWS, 1), F32),
            pltpu.VMEM((8, WIDTH), F32),
            pltpu.VMEM((1, 128), F32),
            pltpu.VMEM((DEVICES, 1, 128), F32),
            dma((2, PAIRS)),
            dma((STRIPS,)),
            dma((3, STRIPS, 3)),
            dma((3, STRIPS, 3)),
            dma((STRIPS,)),
            dma((STRIPS,)),
            dma((DEVICES,)),
            dma((DEVICES,)),
        ],
        compiler_params=pltpu.CompilerParams(
            collective_id=0, has_side_effects=True, vmem_limit_bytes=36 << 20
        ),
    )(lambda_tiles, dressing, constant_term, domain_mask, virtual_energy.reshape(1, V), pair_shift)
    resid = pltpu.with_memory_space_constraint(resid, pltpu.VMEM)
    masked = pltpu.with_memory_space_constraint(masked, pltpu.VMEM)
    out = pl.pallas_call(
        update_kernel,
        name="scale_update",
        out_shape=jax.ShapeDtypeStruct(flat, BF16),
        in_specs=[vmem, vmem, vmem],
        out_specs=hbm,
        scratch_shapes=[pltpu.VMEM(flat, BF16), dma((PAIRS * ROWS // CHUNK,))],
        compiler_params=pltpu.CompilerParams(vmem_limit_bytes=16 << 20),
    )(resid, masked, factor)
    return out.reshape(PAIRS, ROWS, V)


def solution(mesh):
    return jax.shard_map(
        per_device,
        mesh=mesh,
        in_specs=(
            P("row", "col", None),
            P(("row", "col"), None),
            P("row", "col", None),
            P("row", None),
            P(),
            P("row"),
        ),
        out_specs=P("row", "col", None),
        check_vma=False,
    )
```

```python
import jax
import jax.numpy as jnp
from jax import lax
from jax.experimental import pallas as pl
from jax.experimental.pallas import tpu as pltpu
from jax.sharding import PartitionSpec as P

MESH = pl.DeviceIdType.MESH
F32, BF16 = jnp.float32, jnp.bfloat16
TILE = 64
PAIRS, ROWS, V = 6, 256, 2048
WIDTH = 256
STRIPS = V // WIDTH
DEVICES = 128
ENTRIES = 96 * V * V
ORDERS = ("yzx", "xyz", "zxy")
VT = V // TILE
GROUPS = ((0, 1, 2), (3, 4, 5), (6, 7))
STREAMS = ("one", "two", "ring", "relay", "side")


def place():
    row, col = lax.axis_index("row"), lax.axis_index("col")
    return {
        "x": row // 4,
        "zl": (row // 2) % 2,
        "c": row % 2,
        "zh": col // 4,
        "y": col % 4,
        "z": (col // 4) * 2 + (row // 2) % 2,
    }


def device(at):
    return {"row": at["x"] * 4 + (at["z"] % 2) * 2 + at["c"], "col": (at["z"] // 2) * 4 + at["y"]}


def neighbour(at, axis, hops):
    moved = dict(at)
    moved[axis] = (at[axis] + hops) % 4
    return device(moved)


def sibling(at):
    moved = dict(at)
    moved["c"] = 1 - at["c"]
    return device(moved)


def block(gathered, strip, at, whole, half=None):
    every = slice(None)
    x, zl = (every if "x" in whole else at["x"]), (every if "z" in whole else at["zl"])
    if half is not None:
        if "x" in whole:
            x = pl.ds(2 * half, 2)
        else:
            zl = half
    return gathered.at[
        strip,
        x,
        zl,
        every if "z" in whole else at["zh"],
        at["c"],
        every if "y" in whole else at["y"],
    ]


def moved(at, axis, hops):
    there = dict(at)
    there[axis] = (at[axis] + hops) % 4
    if axis == "z":
        there["zl"], there["zh"] = there["z"] % 2, there["z"] // 2
    return there


def gather_kernel(
    lam_hbm, dress_hbm, const_hbm, mask_hbm, energy_hbm, shift_hbm,
    resid_ref, masked_ref, factor_ref,
    gathered, turned, const_ref, mask_ref, energy_ref, shift_ref, colmask, rowmask, squares, mine, everyone,
    small_sem, load_sem, own_sem, send_sem, recv_one, recv_two, recv_ring, recv_relay, recv_side, sum_send, sum_recv,
):
    at = place()
    col = lax.axis_index("col")
    other_core = dict(at, c=1 - at["c"])
    barrier = pltpu.get_barrier_semaphore()
    partners = [device(moved(at, axis, hops)) for axis in "xyz" for hops in (2, 1, 3)] + [device(other_core)]
    for partner in partners:
        pl.semaphore_signal(barrier, inc=1, device_id=partner, device_id_type=MESH)

    own = [
        pltpu.make_async_copy(dress_hbm.at[:, pl.ds(s * WIDTH, WIDTH)], block(gathered, s, at, ""), own_sem)
        for s in range(STRIPS)
    ]
    for copy in own:
        copy.start()
    small = [
        pltpu.make_async_copy(mask_hbm, mask_ref, small_sem.at[0]),
        pltpu.make_async_copy(energy_hbm, energy_ref, small_sem.at[1]),
        pltpu.make_async_copy(shift_hbm, shift_ref, small_sem.at[2]),
    ]
    for copy in small:
        copy.start()
    loads = []
    for p in range(PAIRS):
        rows = pl.ds(p * ROWS, ROWS)
        loads.append(pltpu.make_async_copy(lam_hbm.at[p], masked_ref.at[rows, :], load_sem.at[0, p]))
        loads.append(pltpu.make_async_copy(const_hbm.at[p], const_ref.at[rows, :], load_sem.at[1, p]))
    for copy in loads:
        copy.start()

    def wait_blocks(ref, sem):
        pltpu.make_async_copy(ref, ref, sem).wait()

    wait_blocks(gathered.at[:, 0, 0, 0, 0, 0], own_sem)
    pl.semaphore_wait(barrier, len(partners))

    def send(part, target, stream, recv):
        pltpu.make_async_remote_copy(
            src_ref=part,
            dst_ref=part,
            send_sem=send_sem.at[STREAMS.index(stream)],
            recv_sem=recv,
            device_id=device(target),
            device_id_type=MESH,
        ).start()

    def spread_one(s):
        order = ORDERS[s % 3]
        for hops in (2, 1, 3):
            send(block(gathered, s, at, ""), moved(at, order[0], hops), "one", recv_one)

    def spread_two(s):
        order = ORDERS[s % 3]
        for hops in (2, 1, 3):
            send(block(gathered, s, at, order[0]), moved(at, order[1], hops), "two", recv_two.at[s])

    def spread_ring(s):
        order = ORDERS[s % 3]
        for hops in (1, 3):
            send(block(gathered, s, at, order[:2]), moved(at, order[2], hops), "ring", recv_ring.at[s])
        send(block(gathered, s, at, order[:2]), other_core, "side", recv_side.at[0, s])

    def relay(s):
        order = ORDERS[s % 3]
        wait_blocks(gathered.at[s, 0:2, :, :, 0, :], recv_ring.at[s])
        for hops, half in ((1, 0), (3, 1)):
            source = moved(at, order[2], -hops)
            send(block(gathered, s, source, order[:2], half), moved(at, order[2], hops), "relay", recv_relay.at[s])
        for hops in (1, 3):
            send(block(gathered, s, moved(at, order[2], hops), order[:2]), other_core, "side", recv_side.at[1, s])

    def land(s):
        order = ORDERS[s % 3]
        wait_blocks(gathered.at[s, 0, :, :, 0, :], recv_relay.at[s])
        send(block(gathered, s, moved(at, order[2], 2), order[:2]), other_core, "side", recv_side.at[2, s])

    def ready(s):
        wait_blocks(gathered.at[s, 0, :, :, 0, :], recv_side.at[0, s])
        wait_blocks(gathered.at[s, 0:2, :, :, 0, :], recv_side.at[1, s])
        wait_blocks(gathered.at[s, 0, :, :, 0, :], recv_side.at[2, s])

    for s in range(STRIPS):
        spread_one(s)

    for copy in small:
        copy.wait()
    mask = mask_ref[...].astype(F32)
    tile_of = lax.broadcasted_iota(jnp.int32, (VT, V), 0)
    tile_col = lax.broadcasted_iota(jnp.int32, (VT, V), 1) // TILE
    cols_of = jnp.dot(mask, (tile_of == tile_col).astype(F32), preferred_element_type=F32)
    row_tile = lax.broadcasted_iota(jnp.int32, (ROWS, VT), 0) // TILE + col * (ROWS // TILE)
    row_hot = (row_tile == lax.broadcasted_iota(jnp.int32, (ROWS, VT), 1)).astype(F32)
    for p in range(PAIRS):
        colmask[p] = cols_of[p : p + 1, :]
        rowmask[p] = jnp.sum(row_hot * mask[p : p + 1, :], axis=1, keepdims=True)
    squares[...] = jnp.zeros_like(squares)

    wait_blocks(gathered.at[:, 0:3, 0, 0, 0, 0], recv_one)
    for s in range(STRIPS):
        spread_two(s)

    def prepare(p):
        rows = pl.ds(p * ROWS, ROWS)
        loads[2 * p].wait()
        loads[2 * p + 1].wait()
        for q in range(V // 256):
            cols = pl.ds(q * 256, 256)
            domain = (rowmask[p] * colmask[p, :, cols]).astype(BF16)
            part = masked_ref[rows, cols] * domain
            masked_ref[rows, cols] = part
            pieces = [part[:, k * 64 : (k + 1) * 64] for k in (0, 2, 1, 3)]
            turned[rows, cols] = jnp.concatenate(pieces, axis=1)
            const_ref[rows, cols] = const_ref[rows, cols] * domain

    def arrive_two(s):
        wait_blocks(gathered.at[s, 0:3, 0, 0, 0, :], recv_two.at[s])
        spread_ring(s)

    for p in (0, 1, 2):
        prepare(p)
    for s in GROUPS[0]:
        arrive_two(s)
    for p in (3, 4, 5):
        prepare(p)
    for s in GROUPS[1]:
        arrive_two(s)

    def multiply(first, last):
        def strip(s, carry):
            cols = pl.ds(pl.multiple_of(s * WIDTH, WIDTH), WIDTH)
            right = gathered[s].reshape(V, WIDTH)
            product = jnp.dot(turned[...], right, preferred_element_type=F32)
            total = jnp.zeros((8, WIDTH), F32)
            for p in range(PAIRS):
                rows = pl.ds(p * ROWS, ROWS)
                part = const_ref[rows, cols].astype(F32) + colmask[p, :, cols] * product[p * ROWS : (p + 1) * ROWS, :]
                resid_ref[rows, cols] = part
                total = total + jnp.sum((part * part).reshape(ROWS // 8, 8, WIDTH), axis=0)
            squares[...] += total
            return carry

        lax.fori_loop(first, last, strip, 0)

    for s in GROUPS[0]:
        relay(s)
    for s in GROUPS[2]:
        arrive_two(s)
    for s in GROUPS[1]:
        relay(s)
    for s in GROUPS[0]:
        land(s)
    for s in GROUPS[0]:
        ready(s)
    multiply(0, 2)
    for s in GROUPS[2]:
        relay(s)
    for s in GROUPS[1]:
        land(s)
    multiply(2, 3)
    for s in GROUPS[1]:
        ready(s)
    multiply(3, 5)
    for s in GROUPS[2]:
        land(s)
    multiply(5, 6)
    for s in GROUPS[2]:
        ready(s)
    multiply(6, 8)

    eight = squares[:, :128] + squares[:, 128:]
    mine[...] = jnp.sum(eight, axis=0, keepdims=True)
    me = lax.axis_index("row") * 8 + col

    def tell(step, carry):
        other = (me + step) % DEVICES
        pltpu.make_async_remote_copy(
            src_ref=mine,
            dst_ref=everyone.at[me],
            send_sem=sum_send,
            recv_sem=sum_recv,
            device_id={"row": other // 8, "col": other % 8},
            device_id_type=MESH,
        ).start()
        return carry

    lax.fori_loop(1, DEVICES, tell, 0, unroll=True)
    everyone[me] = mine[...]

    own_energy = energy_ref[:, pl.ds(pl.multiple_of(col * ROWS, ROWS), ROWS)]
    diagonal = lax.broadcasted_iota(jnp.int32, (ROWS, ROWS), 0) == lax.broadcasted_iota(jnp.int32, (ROWS, ROWS), 1)
    energy_rows = jnp.sum(jnp.where(diagonal, own_energy, 0.0), axis=1, keepdims=True)

    def divide(p, carry):
        shifted = energy_rows + shift_ref[p]
        for s in range(STRIPS):
            rows, cols = pl.ds(pl.multiple_of(p * ROWS, ROWS), ROWS), pl.ds(s * WIDTH, WIDTH)
            resid_ref[rows, cols] = resid_ref[rows, cols] / (shifted + energy_ref[:, cols])
        return carry

    lax.fori_loop(0, PAIRS, divide, 0)

    wait_blocks(everyone.at[0 : DEVICES - 1], sum_recv)
    total = jnp.sum(jnp.sum(everyone[...], axis=0), axis=1, keepdims=True)
    factor = 0.25 * lax.rsqrt(total / ENTRIES + 1e-06)
    factor_ref[...] = jnp.zeros((8, 128), F32) + factor

    wait_blocks(gathered.at[:, 0:3, 0, 0, 0, 0], send_sem.at[0])
    wait_blocks(gathered.at[:, 0:3, 0, 0, 0, :], send_sem.at[1])
    wait_blocks(gathered.at[:, :, :, :, 0, 0:2], send_sem.at[2])
    wait_blocks(gathered.at[:, :, :, :, 0, 0], send_sem.at[3])
    wait_blocks(gathered.at[:, :, :, :, 0, :], send_sem.at[4])
    wait_blocks(everyone.at[0 : DEVICES - 1], sum_send)


CHUNK = 128


def update_kernel(resid_ref, masked_ref, factor_ref, out_hbm, staged, sem):
    factor = factor_ref[0:1, 0:1]
    copies = []
    for i in range(PAIRS * ROWS // CHUNK):
        rows = pl.ds(i * CHUNK, CHUNK)
        staged[rows, :] = (masked_ref[rows, :].astype(F32) + factor * resid_ref[rows, :]).astype(BF16)
        copies.append(pltpu.make_async_copy(staged.at[rows, :], out_hbm.at[rows, :], sem.at[i]))
        copies[-1].start()
    for copy in copies:
        copy.wait()


def per_device(lambda_tiles, dressing, constant_term, domain_mask, virtual_energy, pair_shift):
    vmem, hbm = (pl.BlockSpec(memory_space=m) for m in (pltpu.VMEM, pl.ANY))
    flat = (PAIRS * ROWS, V)
    dma = pltpu.SemaphoreType.DMA
    resid, masked, factor = pl.pallas_call(
        gather_kernel,
        name="gather_multiply",
        out_shape=(pltpu.VMEM(flat, F32), pltpu.VMEM(flat, BF16), pltpu.VMEM((8, 128), F32)),
        in_specs=[hbm] * 6,
        out_specs=(vmem, vmem, vmem),
        scratch_shapes=[
            pltpu.VMEM((STRIPS, 4, 2, 2, 2, 4, 16, WIDTH), BF16),
            pltpu.VMEM(flat, BF16),
            pltpu.VMEM(flat, BF16),
            pltpu.VMEM((PAIRS, VT), jnp.int32),
            pltpu.VMEM((1, V), F32),
            pltpu.SMEM((PAIRS,), F32),
            pltpu.VMEM((PAIRS, 1, V), F32),
            pltpu.VMEM((PAIRS, ROWS, 1), F32),
            pltpu.VMEM((8, WIDTH), F32),
            pltpu.VMEM((1, 128), F32),
            pltpu.VMEM((DEVICES, 1, 128), F32),
            dma((3,)),
            dma((2, PAIRS)),
            dma,
            dma((len(STREAMS),)),
            dma,
            dma((STRIPS,)),
            dma((STRIPS,)),
            dma((STRIPS,)),
            dma((3, STRIPS)),
            dma,
            dma,
        ],
        compiler_params=pltpu.CompilerParams(
            collective_id=0, has_side_effects=True, vmem_limit_bytes=36 << 20
        ),
    )(lambda_tiles, dressing, constant_term, domain_mask, virtual_energy.reshape(1, V), pair_shift)
    resid = pltpu.with_memory_space_constraint(resid, pltpu.VMEM)
    masked = pltpu.with_memory_space_constraint(masked, pltpu.VMEM)
    out = pl.pallas_call(
        update_kernel,
        name="scale_update",
        out_shape=jax.ShapeDtypeStruct(flat, BF16),
        in_specs=[vmem, vmem, vmem],
        out_specs=hbm,
        scratch_shapes=[pltpu.VMEM(flat, BF16), dma((PAIRS * ROWS // CHUNK,))],
        compiler_params=pltpu.CompilerParams(vmem_limit_bytes=16 << 20),
    )(resid, masked, factor)
    return out.reshape(PAIRS, ROWS, V)


def solution(mesh):
    return jax.shard_map(
        per_device,
        mesh=mesh,
        in_specs=(
            P("row", "col", None),
            P(("row", "col"), None),
            P("row", "col", None),
            P("row", None),
            P(),
            P("row"),
        ),
        out_specs=P("row", "col", None),
        check_vma=False,
    )
```

```python
import jax
import jax.numpy as jnp
from jax import lax
from jax.experimental import pallas as pl
from jax.experimental.pallas import tpu as pltpu
from jax.sharding import PartitionSpec as P

MESH = pl.DeviceIdType.MESH
F32, BF16 = jnp.float32, jnp.bfloat16
TILE = 64
PAIRS, ROWS, V = 6, 256, 2048
WIDTH = 256
STRIPS = V // WIDTH
DEVICES = 128
ENTRIES = 96 * V * V
ORDERS = ("yzx", "xyz", "zxy", "yzx", "xyz", "zxy", "yzx", "xyz")
VT = V // TILE
GROUPS = ((0, 1, 2), (3, 4, 5), (6, 7))
MTILE = 1536
AHEAD = 2
STREAMS = ("one", "two", "ring", "relay", "side")


def place():
    row, col = lax.axis_index("row"), lax.axis_index("col")
    return {
        "x": row // 4,
        "zl": (row // 2) % 2,
        "c": row % 2,
        "zh": col // 4,
        "y": col % 4,
        "z": (col // 4) * 2 + (row // 2) % 2,
    }


def device(at):
    return {"row": at["x"] * 4 + (at["z"] % 2) * 2 + at["c"], "col": (at["z"] // 2) * 4 + at["y"]}


def block(gathered, strip, at, whole, half=None):
    every = slice(None)
    x, zl = (every if "x" in whole else at["x"]), (every if "z" in whole else at["zl"])
    if half is not None:
        if "x" in whole:
            x = pl.ds(2 * half, 2)
        else:
            zl = half
    return gathered.at[
        strip,
        x,
        zl,
        every if "z" in whole else at["zh"],
        at["c"],
        every if "y" in whole else at["y"],
    ]


def moved(at, axis, hops):
    there = dict(at)
    there[axis] = (at[axis] + hops) % 4
    if axis == "z":
        there["zl"], there["zh"] = there["z"] % 2, there["z"] // 2
    return there


def gather_kernel(
    lam_hbm, dress_hbm, const_hbm, mask_hbm, energy_hbm, shift_hbm,
    resid_ref, masked_ref, factor_ref,
    gathered, turned, const_ref, mask_ref, energy_ref, shift_ref, colmask, rowmask, squares, mine, everyone,
    small_sem, load_sem, own_sem, send_sem, recv_one, recv_two, recv_ring, recv_relay, recv_side, sum_send, sum_recv,
):
    at = place()
    col = lax.axis_index("col")
    other_core = dict(at, c=1 - at["c"])
    barrier = pltpu.get_barrier_semaphore()
    partners = [device(moved(at, axis, hops)) for axis in "xyz" for hops in (2, 1, 3)] + [device(other_core)]
    for partner in partners:
        pl.semaphore_signal(barrier, inc=1, device_id=partner, device_id_type=MESH)

    own = [
        pltpu.make_async_copy(dress_hbm.at[:, pl.ds(s * WIDTH, WIDTH)], block(gathered, s, at, ""), own_sem)
        for s in range(STRIPS)
    ]
    for copy in own:
        copy.start()
    small = [
        pltpu.make_async_copy(mask_hbm, mask_ref, small_sem.at[0]),
        pltpu.make_async_copy(energy_hbm, energy_ref, small_sem.at[1]),
        pltpu.make_async_copy(shift_hbm, shift_ref, small_sem.at[2]),
    ]
    for copy in small:
        copy.start()
    def load(p):
        rows = pl.ds(pl.multiple_of(p * ROWS, ROWS), ROWS)
        pltpu.make_async_copy(lam_hbm.at[p], masked_ref.at[rows, :], load_sem.at[0, p]).start()
        pltpu.make_async_copy(const_hbm.at[p], const_ref.at[rows, :], load_sem.at[1, p]).start()

    def wait_blocks(ref, sem):
        pltpu.make_async_copy(ref, ref, sem).wait()

    pl.semaphore_wait(barrier, len(partners))

    def send(part, target, stream, recv, source=None):
        pltpu.make_async_remote_copy(
            src_ref=part if source is None else source,
            dst_ref=part,
            send_sem=send_sem.at[STREAMS.index(stream)],
            recv_sem=recv,
            device_id=device(target),
            device_id_type=MESH,
        ).start()

    def spread_one(s):
        order = ORDERS[s]
        for hops in (2, 1, 3):
            source = dress_hbm.at[:, pl.ds(s * WIDTH, WIDTH)]
            send(block(gathered, s, at, ""), moved(at, order[0], hops), "one", recv_one, source)

    def spread_two(s):
        order = ORDERS[s]
        for hops in (2, 1, 3):
            send(block(gathered, s, at, order[0]), moved(at, order[1], hops), "two", recv_two.at[s])

    def spread_ring(s):
        order = ORDERS[s]
        for hops in (1, 3):
            send(block(gathered, s, at, order[:2]), moved(at, order[2], hops), "ring", recv_ring.at[s])
        send(block(gathered, s, at, order[:2]), other_core, "side", recv_side.at[0, s])

    def relay(s):
        order = ORDERS[s]
        wait_blocks(gathered.at[s, 0:2, :, :, 0, :], recv_ring.at[s])
        for hops, half in ((1, 0), (3, 1)):
            source = moved(at, order[2], -hops)
            send(block(gathered, s, source, order[:2], half), moved(at, order[2], hops), "relay", recv_relay.at[s])
        for hops in (1, 3):
            send(block(gathered, s, moved(at, order[2], hops), order[:2]), other_core, "side", recv_side.at[1, s])

    def land(s):
        order = ORDERS[s]
        wait_blocks(gathered.at[s, 0, :, :, 0, :], recv_relay.at[s])
        send(block(gathered, s, moved(at, order[2], 2), order[:2]), other_core, "side", recv_side.at[2, s])

    def ready(s):
        wait_blocks(gathered.at[s, 0, :, :, 0, :], recv_side.at[0, s])
        wait_blocks(gathered.at[s, 0:2, :, :, 0, :], recv_side.at[1, s])
        wait_blocks(gathered.at[s, 0, :, :, 0, :], recv_side.at[2, s])

    for s in range(STRIPS):
        spread_one(s)

    for copy in small:
        copy.wait()
    mask = mask_ref[...].astype(F32)
    tile_of = lax.broadcasted_iota(jnp.int32, (VT, V), 0)
    tile_col = lax.broadcasted_iota(jnp.int32, (VT, V), 1) // TILE
    cols_of = jnp.dot(mask, (tile_of == tile_col).astype(F32), preferred_element_type=F32)
    row_tile = lax.broadcasted_iota(jnp.int32, (ROWS, VT), 0) // TILE + col * (ROWS // TILE)
    row_hot = (row_tile == lax.broadcasted_iota(jnp.int32, (ROWS, VT), 1)).astype(F32)
    for p in range(PAIRS):
        colmask[p] = cols_of[p : p + 1, :]
        rowmask[p] = jnp.sum(row_hot * mask[p : p + 1, :], axis=1, keepdims=True)
    squares[...] = jnp.zeros_like(squares)

    wait_blocks(gathered.at[:, 0, 0, 0, 0, 0], own_sem)
    wait_blocks(gathered.at[:, 0:3, 0, 0, 0, 0], recv_one)
    for s in range(STRIPS):
        spread_two(s)

    def prepare(p, carry):
        rows = pl.ds(pl.multiple_of(p * ROWS, ROWS), ROWS)
        for ref, k in ((masked_ref, 0), (const_ref, 1)):
            pltpu.make_async_copy(ref.at[rows, :], ref.at[rows, :], load_sem.at[k, p]).wait()

        @pl.when(p + AHEAD < PAIRS)
        def _():
            load(p + AHEAD)

        for q in range(V // 256):
            cols = pl.ds(q * 256, 256)
            domain = (rowmask[p] * colmask[p, :, cols]).astype(BF16)
            part = masked_ref[rows, cols] * domain
            masked_ref[rows, cols] = part
            pieces = [part[:, k * 64 : (k + 1) * 64] for k in (0, 2, 1, 3)]
            turned[rows, cols] = jnp.concatenate(pieces, axis=1)
            const_ref[rows, cols] = const_ref[rows, cols] * domain
        return carry

    def arrive_two(s):
        wait_blocks(gathered.at[s, 0:3, 0, 0, 0, :], recv_two.at[s])
        spread_ring(s)

    for s in GROUPS[0]:
        arrive_two(s)
    for p in range(AHEAD):
        load(p)
    for s in GROUPS[1]:
        arrive_two(s)
    lax.fori_loop(0, PAIRS, prepare, 0)
    for s in GROUPS[0]:
        relay(s)
    for s in GROUPS[2]:
        arrive_two(s)
    for s in GROUPS[1]:
        relay(s)
    for s in GROUPS[0]:
        land(s)

    def strip(s, carry):
        @pl.when(s == 1)
        def _():
            for later in GROUPS[2]:
                relay(later)
            for later in GROUPS[1]:
                land(later)

        @pl.when(s == 4)
        def _():
            for later in GROUPS[2]:
                land(later)

        ready(s)
        cols = pl.ds(pl.multiple_of(s * WIDTH, WIDTH), WIDTH)

        def rows_of(i, carry):
            rows = pl.ds(pl.multiple_of(i * MTILE, MTILE), MTILE)
            product = jnp.dot(turned[rows, :], gathered[s].reshape(V, WIDTH), preferred_element_type=F32)
            total = jnp.zeros((8, WIDTH), F32)
            for q in range(MTILE // ROWS):
                p = i * (MTILE // ROWS) + q
                pair_rows = pl.ds(pl.multiple_of(p * ROWS, ROWS), ROWS)
                part = const_ref[pair_rows, cols].astype(F32) + colmask[p, :, cols] * product[q * ROWS : (q + 1) * ROWS, :]
                resid_ref[pair_rows, cols] = part
                total = total + jnp.sum((part * part).reshape(ROWS // 8, 8, WIDTH), axis=0)
            squares[...] += total
            return carry

        lax.fori_loop(0, PAIRS * ROWS // MTILE, rows_of, 0)
        return carry

    lax.fori_loop(0, STRIPS, strip, 0)

    eight = squares[:, :128] + squares[:, 128:]
    mine[...] = jnp.sum(eight, axis=0, keepdims=True)
    me = lax.axis_index("row") * 8 + col

    offsets = [(dx, dy, dz, dc) for dx in range(4) for dy in range(4) for dz in range(4) for dc in range(2)][1:]
    offsets.sort(key=lambda o: (-sum(min(d, 4 - d) for d in o[:3]), o))
    xs, ys, zs = ([(at[a] + d) % 4 for d in range(4)] for a in "xyz")
    row_parts = [[x * 4 + (z % 2) * 2 for z in zs] for x in xs]
    col_parts = [[(z // 2) * 4 + y for z in zs] for y in ys]
    for dx, dy, dz, dc in offsets:
        core = at["c"] if dc == 0 else other_core["c"]
        pltpu.make_async_remote_copy(
            src_ref=mine,
            dst_ref=everyone.at[me],
            send_sem=sum_send,
            recv_sem=sum_recv,
            device_id={"row": row_parts[dx][dz] + core, "col": col_parts[dy][dz]},
            device_id_type=MESH,
        ).start()
    everyone[me] = mine[...]

    own_energy = energy_ref[:, pl.ds(pl.multiple_of(col * ROWS, ROWS), ROWS)]
    diagonal = lax.broadcasted_iota(jnp.int32, (ROWS, ROWS), 0) == lax.broadcasted_iota(jnp.int32, (ROWS, ROWS), 1)
    energy_rows = jnp.sum(jnp.where(diagonal, own_energy, 0.0), axis=1, keepdims=True)

    def divide(p, carry):
        shifted = energy_rows + shift_ref[p]
        for s in range(STRIPS):
            rows, cols = pl.ds(pl.multiple_of(p * ROWS, ROWS), ROWS), pl.ds(s * WIDTH, WIDTH)
            resid_ref[rows, cols] = resid_ref[rows, cols] / (shifted + energy_ref[:, cols])
        return carry

    lax.fori_loop(0, PAIRS, divide, 0)

    wait_blocks(everyone.at[0 : DEVICES - 1], sum_recv)
    total = jnp.sum(jnp.sum(everyone[...], axis=0), axis=1, keepdims=True)
    factor = 0.25 * lax.rsqrt(total / ENTRIES + 1e-06)
    factor_ref[...] = jnp.zeros((8, 128), F32) + factor

    wait_blocks(gathered.at[:, 0:3, 0, 0, 0, 0], send_sem.at[0])
    wait_blocks(gathered.at[:, 0:3, 0, 0, 0, :], send_sem.at[1])
    wait_blocks(gathered.at[:, :, :, :, 0, 0:2], send_sem.at[2])
    wait_blocks(gathered.at[:, :, :, :, 0, 0], send_sem.at[3])
    wait_blocks(gathered.at[:, :, :, :, 0, :], send_sem.at[4])
    wait_blocks(everyone.at[0 : DEVICES - 1], sum_send)


CHUNK = 128


def update_kernel(resid_ref, masked_ref, factor_ref, out_hbm, staged, sem):
    factor = factor_ref[0:1, 0:1]
    copies = []
    for i in range(PAIRS * ROWS // CHUNK):
        rows = pl.ds(i * CHUNK, CHUNK)
        staged[rows, :] = (masked_ref[rows, :].astype(F32) + factor * resid_ref[rows, :]).astype(BF16)
        copies.append(pltpu.make_async_copy(staged.at[rows, :], out_hbm.at[rows, :], sem.at[i]))
        copies[-1].start()
    for copy in copies:
        copy.wait()


def per_device(lambda_tiles, dressing, constant_term, domain_mask, virtual_energy, pair_shift):
    vmem, hbm = (pl.BlockSpec(memory_space=m) for m in (pltpu.VMEM, pl.ANY))
    flat = (PAIRS * ROWS, V)
    dma = pltpu.SemaphoreType.DMA
    resid, masked, factor = pl.pallas_call(
        gather_kernel,
        name="gather_multiply",
        out_shape=(pltpu.VMEM(flat, F32), pltpu.VMEM(flat, BF16), pltpu.VMEM((8, 128), F32)),
        in_specs=[hbm] * 6,
        out_specs=(vmem, vmem, vmem),
        scratch_shapes=[
            pltpu.VMEM((STRIPS, 4, 2, 2, 2, 4, 16, WIDTH), BF16),
            pltpu.VMEM(flat, BF16),
            pltpu.VMEM(flat, BF16),
            pltpu.VMEM((PAIRS, VT), jnp.int32),
            pltpu.VMEM((1, V), F32),
            pltpu.SMEM((PAIRS,), F32),
            pltpu.VMEM((PAIRS, 1, V), F32),
            pltpu.VMEM((PAIRS, ROWS, 1), F32),
            pltpu.VMEM((8, WIDTH), F32),
            pltpu.VMEM((1, 128), F32),
            pltpu.VMEM((DEVICES, 1, 128), F32),
            dma((3,)),
            dma((2, PAIRS)),
            dma,
            dma((len(STREAMS),)),
            dma,
            dma((STRIPS,)),
            dma((STRIPS,)),
            dma((STRIPS,)),
            dma((3, STRIPS)),
            dma,
            dma,
        ],
        compiler_params=pltpu.CompilerParams(
            collective_id=0, has_side_effects=True, vmem_limit_bytes=36 << 20
        ),
    )(lambda_tiles, dressing, constant_term, domain_mask, virtual_energy.reshape(1, V), pair_shift)
    resid = pltpu.with_memory_space_constraint(resid, pltpu.VMEM)
    masked = pltpu.with_memory_space_constraint(masked, pltpu.VMEM)
    out = pl.pallas_call(
        update_kernel,
        name="scale_update",
        out_shape=jax.ShapeDtypeStruct(flat, BF16),
        in_specs=[vmem, vmem, vmem],
        out_specs=hbm,
        scratch_shapes=[pltpu.VMEM(flat, BF16), dma((PAIRS * ROWS // CHUNK,))],
        compiler_params=pltpu.CompilerParams(vmem_limit_bytes=16 << 20),
    )(resid, masked, factor)
    return out.reshape(PAIRS, ROWS, V)


def solution(mesh):
    return jax.shard_map(
        per_device,
        mesh=mesh,
        in_specs=(
            P("row", "col", None),
            P(("row", "col"), None),
            P("row", "col", None),
            P("row", None),
            P(),
            P("row"),
        ),
        out_specs=P("row", "col", None),
        check_vma=False,
    )
```

```python
import jax
import jax.numpy as jnp
from jax import lax
from jax.experimental import pallas as pl
from jax.experimental.pallas import tpu as pltpu
from jax.sharding import PartitionSpec as P

MESH = pl.DeviceIdType.MESH
F32, BF16 = jnp.float32, jnp.bfloat16
TILE = 64
PAIRS, ROWS, V = 6, 256, 2048
WIDTH = 256
STRIPS = V // WIDTH
DEVICES = 128
ENTRIES = 96 * V * V
ORDERS = ("yzx", "xyz", "zxy", "yzx", "xyz", "zxy", "yzx", "xyz")
VT = V // TILE
GROUPS = ((0, 1, 2), (3, 4, 5), (6, 7))
MTILE = 1536
AHEAD = 2
STREAMS = ("one", "two", "ring", "relay", "side")


def place():
    row, col = lax.axis_index("row"), lax.axis_index("col")
    return {
        "x": row // 4,
        "zl": (row // 2) % 2,
        "c": row % 2,
        "zh": col // 4,
        "y": col % 4,
        "z": (col // 4) * 2 + (row // 2) % 2,
    }


def device(at):
    return {"row": at["x"] * 4 + (at["z"] % 2) * 2 + at["c"], "col": (at["z"] // 2) * 4 + at["y"]}


def block(gathered, strip, at, whole, half=None):
    every = slice(None)
    x, zl = (every if "x" in whole else at["x"]), (every if "z" in whole else at["zl"])
    if half is not None:
        if "x" in whole:
            x = pl.ds(2 * half, 2)
        else:
            zl = half
    return gathered.at[
        strip,
        x,
        zl,
        every if "z" in whole else at["zh"],
        at["c"],
        every if "y" in whole else at["y"],
    ]


def moved(at, axis, hops):
    there = dict(at)
    there[axis] = (at[axis] + hops) % 4
    if axis == "z":
        there["zl"], there["zh"] = there["z"] % 2, there["z"] // 2
    return there


def gather_kernel(
    lam_hbm, dress_hbm, const_hbm, mask_hbm, energy_hbm, shift_hbm,
    resid_ref, masked_ref, factor_ref,
    gathered, turned, const_ref, mask_ref, energy_ref, shift_ref, colmask, rowmask, squares, mine, everyone,
    small_sem, load_sem, own_sem, send_sem, recv_one, recv_two, recv_ring, recv_relay, recv_side, sum_send, sum_recv,
):
    at = place()
    col = lax.axis_index("col")
    other_core = dict(at, c=1 - at["c"])
    barrier = pltpu.get_barrier_semaphore()
    partners = [device(moved(at, axis, hops)) for axis in "xyz" for hops in (2, 1, 3)] + [device(other_core)]
    for partner in partners:
        pl.semaphore_signal(barrier, inc=1, device_id=partner, device_id_type=MESH)

    own = [
        pltpu.make_async_copy(dress_hbm.at[:, pl.ds(s * WIDTH, WIDTH)], block(gathered, s, at, ""), own_sem)
        for s in range(STRIPS)
    ]
    for copy in own:
        copy.start()
    small = [
        pltpu.make_async_copy(mask_hbm, mask_ref, small_sem.at[0]),
        pltpu.make_async_copy(energy_hbm, energy_ref, small_sem.at[1]),
        pltpu.make_async_copy(shift_hbm, shift_ref, small_sem.at[2]),
    ]
    for copy in small:
        copy.start()
    def load(p):
        rows = pl.ds(pl.multiple_of(p * ROWS, ROWS), ROWS)
        pltpu.make_async_copy(lam_hbm.at[p], masked_ref.at[rows, :], load_sem.at[0, p]).start()
        pltpu.make_async_copy(const_hbm.at[p], const_ref.at[rows, :], load_sem.at[1, p]).start()

    def wait_blocks(ref, sem):
        pltpu.make_async_copy(ref, ref, sem).wait()

    pl.semaphore_wait(barrier, len(partners))

    def send(part, target, stream, recv, source=None):
        pltpu.make_async_remote_copy(
            src_ref=part if source is None else source,
            dst_ref=part,
            send_sem=send_sem.at[STREAMS.index(stream)],
            recv_sem=recv,
            device_id=device(target),
            device_id_type=MESH,
        ).start()

    def spread_one(s):
        order = ORDERS[s]
        for hops in (2, 1, 3):
            source = dress_hbm.at[:, pl.ds(s * WIDTH, WIDTH)]
            send(block(gathered, s, at, ""), moved(at, order[0], hops), "one", recv_one, source)

    def spread_two(s):
        order = ORDERS[s]
        for hops in (2, 1, 3):
            send(block(gathered, s, at, order[0]), moved(at, order[1], hops), "two", recv_two.at[s])

    def spread_ring(s):
        order = ORDERS[s]
        for hops in (1, 3):
            send(block(gathered, s, at, order[:2]), moved(at, order[2], hops), "ring", recv_ring.at[s])
        send(block(gathered, s, at, order[:2]), other_core, "side", recv_side.at[0, s])

    def relay(s):
        order = ORDERS[s]
        wait_blocks(gathered.at[s, 0:2, :, :, 0, :], recv_ring.at[s])
        for hops, half in ((1, 0), (3, 1)):
            source = moved(at, order[2], -hops)
            send(block(gathered, s, source, order[:2], half), moved(at, order[2], hops), "relay", recv_relay.at[s])
        for hops in (1, 3):
            send(block(gathered, s, moved(at, order[2], hops), order[:2]), other_core, "side", recv_side.at[1, s])

    def land(s):
        order = ORDERS[s]
        wait_blocks(gathered.at[s, 0, :, :, 0, :], recv_relay.at[s])
        send(block(gathered, s, moved(at, order[2], 2), order[:2]), other_core, "side", recv_side.at[2, s])

    def ready(s):
        wait_blocks(gathered.at[s, 0, :, :, 0, :], recv_side.at[0, s])
        wait_blocks(gathered.at[s, 0:2, :, :, 0, :], recv_side.at[1, s])
        wait_blocks(gathered.at[s, 0, :, :, 0, :], recv_side.at[2, s])

    for s in range(STRIPS):
        spread_one(s)

    for copy in small:
        copy.wait()
    mask = mask_ref[...].astype(F32)
    tile_of = lax.broadcasted_iota(jnp.int32, (VT, V), 0)
    tile_col = lax.broadcasted_iota(jnp.int32, (VT, V), 1) // TILE
    cols_of = jnp.dot(mask, (tile_of == tile_col).astype(F32), preferred_element_type=F32)
    row_tile = lax.broadcasted_iota(jnp.int32, (ROWS, VT), 0) // TILE + col * (ROWS // TILE)
    row_hot = (row_tile == lax.broadcasted_iota(jnp.int32, (ROWS, VT), 1)).astype(F32)
    for p in range(PAIRS):
        colmask[p] = cols_of[p : p + 1, :]
        rowmask[p] = jnp.sum(row_hot * mask[p : p + 1, :], axis=1, keepdims=True)
    squares[...] = jnp.zeros_like(squares)

    wait_blocks(gathered.at[:, 0, 0, 0, 0, 0], own_sem)
    wait_blocks(gathered.at[:, 0:3, 0, 0, 0, 0], recv_one)
    for s in range(STRIPS):
        spread_two(s)

    def prepare(p, carry):
        rows = pl.ds(pl.multiple_of(p * ROWS, ROWS), ROWS)
        for ref, k in ((masked_ref, 0), (const_ref, 1)):
            pltpu.make_async_copy(ref.at[rows, :], ref.at[rows, :], load_sem.at[k, p]).wait()

        @pl.when(p + AHEAD < PAIRS)
        def _():
            load(p + AHEAD)

        for q in range(V // 256):
            cols = pl.ds(q * 256, 256)
            domain = (rowmask[p] * colmask[p, :, cols]).astype(BF16)
            part = masked_ref[rows, cols] * domain
            masked_ref[rows, cols] = part
            pieces = [part[:, k * 64 : (k + 1) * 64] for k in (0, 2, 1, 3)]
            turned[rows, cols] = jnp.concatenate(pieces, axis=1)
            const_ref[rows, cols] = const_ref[rows, cols] * domain
        return carry

    def arrive_two(s):
        wait_blocks(gathered.at[s, 0:3, 0, 0, 0, :], recv_two.at[s])
        spread_ring(s)

    for s in GROUPS[0]:
        arrive_two(s)
    for p in range(AHEAD):
        load(p)
    for s in GROUPS[1]:
        arrive_two(s)
    lax.fori_loop(0, PAIRS, prepare, 0)

    def plane_product(s, axis, hops):
        there = moved(at, axis, hops)
        if axis == "x":
            left = turned[:, pl.ds(pl.multiple_of(there["x"] * 512, 512), 512)]
            right = gathered[s, there["x"]]
        else:
            offset = there["zl"] * 256 + there["zh"] * 128
            pieces = [turned[:, pl.ds(pl.multiple_of(x * 512 + offset, 128), 128)] for x in range(4)]
            left = jnp.concatenate(pieces, axis=1)
            right = gathered[s, :, there["zl"], there["zh"]]
        return jnp.dot(left, right.reshape(512, WIDTH), preferred_element_type=F32)

    def near(s, axis):
        cols = pl.ds(s * WIDTH, WIDTH)
        wait_blocks(gathered.at[s, 0, :, :, 0, :], recv_side.at[0, s])
        resid_ref[:, cols] = const_ref[:, cols].astype(F32) + plane_product(s, axis, 0)

    def beside(s, axis):
        cols = pl.ds(s * WIDTH, WIDTH)
        wait_blocks(gathered.at[s, 0:2, :, :, 0, :], recv_side.at[1, s])

        def add(k, carry):
            resid_ref[:, cols] += plane_product(s, axis, 2 * k + 1)
            return carry

        lax.fori_loop(0, 2, add, 0)

    def far(s, axis):
        cols = pl.ds(s * WIDTH, WIDTH)
        wait_blocks(gathered.at[s, 0, :, :, 0, :], recv_side.at[2, s])
        product = plane_product(s, axis, 2)
        total = jnp.zeros((8, WIDTH), F32)
        for p in range(PAIRS):
            rows = pl.ds(p * ROWS, ROWS)
            part = colmask[p, :, cols] * (resid_ref[rows, cols] + product[p * ROWS : (p + 1) * ROWS, :])
            resid_ref[rows, cols] = part
            total = total + jnp.sum((part * part).reshape(ROWS // 8, 8, WIDTH), axis=0)
        squares[...] += total

    for s in GROUPS[0]:
        relay(s)
    for s in GROUPS[2]:
        arrive_two(s)
    near(0, "x")
    near(1, "z")
    for s in GROUPS[1]:
        relay(s)
    beside(0, "x")
    beside(1, "z")
    for s in GROUPS[0]:
        land(s)
    far(0, "x")
    far(1, "z")

    def strip(s, carry):
        @pl.when(s == 2)
        def _():
            for later in GROUPS[2]:
                relay(later)
            for later in GROUPS[1]:
                land(later)

        @pl.when(s == 4)
        def _():
            for later in GROUPS[2]:
                land(later)

        ready(s)
        cols = pl.ds(pl.multiple_of(s * WIDTH, WIDTH), WIDTH)

        def rows_of(i, carry):
            rows = pl.ds(pl.multiple_of(i * MTILE, MTILE), MTILE)
            product = jnp.dot(turned[rows, :], gathered[s].reshape(V, WIDTH), preferred_element_type=F32)
            total = jnp.zeros((8, WIDTH), F32)
            for q in range(MTILE // ROWS):
                p = i * (MTILE // ROWS) + q
                pair_rows = pl.ds(pl.multiple_of(p * ROWS, ROWS), ROWS)
                part = const_ref[pair_rows, cols].astype(F32) + colmask[p, :, cols] * product[q * ROWS : (q + 1) * ROWS, :]
                resid_ref[pair_rows, cols] = part
                total = total + jnp.sum((part * part).reshape(ROWS // 8, 8, WIDTH), axis=0)
            squares[...] += total
            return carry

        lax.fori_loop(0, PAIRS * ROWS // MTILE, rows_of, 0)
        return carry

    lax.fori_loop(2, STRIPS, strip, 0)

    eight = squares[:, :128] + squares[:, 128:]
    mine[...] = jnp.sum(eight, axis=0, keepdims=True)
    me = lax.axis_index("row") * 8 + col

    offsets = [(dx, dy, dz, dc) for dx in range(4) for dy in range(4) for dz in range(4) for dc in range(2)][1:]
    offsets.sort(key=lambda o: (-sum(min(d, 4 - d) for d in o[:3]), o))
    xs, ys, zs = ([(at[a] + d) % 4 for d in range(4)] for a in "xyz")
    row_parts = [[x * 4 + (z % 2) * 2 for z in zs] for x in xs]
    col_parts = [[(z // 2) * 4 + y for z in zs] for y in ys]
    for dx, dy, dz, dc in offsets:
        core = at["c"] if dc == 0 else other_core["c"]
        pltpu.make_async_remote_copy(
            src_ref=mine,
            dst_ref=everyone.at[me],
            send_sem=sum_send,
            recv_sem=sum_recv,
            device_id={"row": row_parts[dx][dz] + core, "col": col_parts[dy][dz]},
            device_id_type=MESH,
        ).start()
    everyone[me] = mine[...]

    own_energy = energy_ref[:, pl.ds(pl.multiple_of(col * ROWS, ROWS), ROWS)]
    diagonal = lax.broadcasted_iota(jnp.int32, (ROWS, ROWS), 0) == lax.broadcasted_iota(jnp.int32, (ROWS, ROWS), 1)
    energy_rows = jnp.sum(jnp.where(diagonal, own_energy, 0.0), axis=1, keepdims=True)

    def divide(p, carry):
        shifted = energy_rows + shift_ref[p]
        for s in range(STRIPS):
            rows, cols = pl.ds(pl.multiple_of(p * ROWS, ROWS), ROWS), pl.ds(s * WIDTH, WIDTH)
            resid_ref[rows, cols] = resid_ref[rows, cols] / (shifted + energy_ref[:, cols])
        return carry

    lax.fori_loop(0, PAIRS, divide, 0)

    wait_blocks(everyone.at[0 : DEVICES - 1], sum_recv)
    total = jnp.sum(jnp.sum(everyone[...], axis=0), axis=1, keepdims=True)
    factor = 0.25 * lax.rsqrt(total / ENTRIES + 1e-06)
    factor_ref[...] = jnp.zeros((8, 128), F32) + factor

    wait_blocks(gathered.at[:, 0:3, 0, 0, 0, 0], send_sem.at[0])
    wait_blocks(gathered.at[:, 0:3, 0, 0, 0, :], send_sem.at[1])
    wait_blocks(gathered.at[:, :, :, :, 0, 0:2], send_sem.at[2])
    wait_blocks(gathered.at[:, :, :, :, 0, 0], send_sem.at[3])
    wait_blocks(gathered.at[:, :, :, :, 0, :], send_sem.at[4])
    wait_blocks(everyone.at[0 : DEVICES - 1], sum_send)


CHUNK = 64


def update_kernel(resid_ref, masked_ref, factor_ref, out_hbm, staged, sem):
    factor = factor_ref[0:1, 0:1]
    copies = []
    for i in range(PAIRS * ROWS // CHUNK):
        rows = pl.ds(i * CHUNK, CHUNK)
        staged[rows, :] = (masked_ref[rows, :].astype(F32) + factor * resid_ref[rows, :]).astype(BF16)
        copies.append(pltpu.make_async_copy(staged.at[rows, :], out_hbm.at[rows, :], sem.at[i]))
        copies[-1].start()
    for copy in copies:
        copy.wait()


def per_device(lambda_tiles, dressing, constant_term, domain_mask, virtual_energy, pair_shift):
    vmem, hbm = (pl.BlockSpec(memory_space=m) for m in (pltpu.VMEM, pl.ANY))
    flat = (PAIRS * ROWS, V)
    dma = pltpu.SemaphoreType.DMA
    resid, masked, factor = pl.pallas_call(
        gather_kernel,
        name="gather_multiply",
        out_shape=(pltpu.VMEM(flat, F32), pltpu.VMEM(flat, BF16), pltpu.VMEM((8, 128), F32)),
        in_specs=[hbm] * 6,
        out_specs=(vmem, vmem, vmem),
        scratch_shapes=[
            pltpu.VMEM((STRIPS, 4, 2, 2, 2, 4, 16, WIDTH), BF16),
            pltpu.VMEM(flat, BF16),
            pltpu.VMEM(flat, BF16),
            pltpu.VMEM((PAIRS, VT), jnp.int32),
            pltpu.VMEM((1, V), F32),
            pltpu.SMEM((PAIRS,), F32),
            pltpu.VMEM((PAIRS, 1, V), F32),
            pltpu.VMEM((PAIRS, ROWS, 1), F32),
            pltpu.VMEM((8, WIDTH), F32),
            pltpu.VMEM((1, 128), F32),
            pltpu.VMEM((DEVICES, 1, 128), F32),
            dma((3,)),
            dma((2, PAIRS)),
            dma,
            dma((len(STREAMS),)),
            dma,
            dma((STRIPS,)),
            dma((STRIPS,)),
            dma((STRIPS,)),
            dma((3, STRIPS)),
            dma,
            dma,
        ],
        compiler_params=pltpu.CompilerParams(
            collective_id=0, has_side_effects=True, vmem_limit_bytes=36 << 20
        ),
    )(lambda_tiles, dressing, constant_term, domain_mask, virtual_energy.reshape(1, V), pair_shift)
    resid = pltpu.with_memory_space_constraint(resid, pltpu.VMEM)
    masked = pltpu.with_memory_space_constraint(masked, pltpu.VMEM)
    out = pl.pallas_call(
        update_kernel,
        name="scale_update",
        out_shape=jax.ShapeDtypeStruct(flat, BF16),
        in_specs=[vmem, vmem, vmem],
        out_specs=hbm,
        scratch_shapes=[pltpu.VMEM(flat, BF16), dma((PAIRS * ROWS // CHUNK,))],
        compiler_params=pltpu.CompilerParams(vmem_limit_bytes=16 << 20),
    )(resid, masked, factor)
    return out.reshape(PAIRS, ROWS, V)


def solution(mesh):
    return jax.shard_map(
        per_device,
        mesh=mesh,
        in_specs=(
            P("row", "col", None),
            P(("row", "col"), None),
            P("row", "col", None),
            P("row", None),
            P(),
            P("row"),
        ),
        out_specs=P("row", "col", None),
        check_vma=False,
    )
```

```python
import jax
import jax.numpy as jnp
from jax import lax
from jax.experimental import pallas as pl
from jax.experimental.pallas import tpu as pltpu
from jax.sharding import PartitionSpec as P

MESH = pl.DeviceIdType.MESH
F32, BF16 = jnp.float32, jnp.bfloat16
TILE = 64
PAIRS, ROWS, V = 6, 256, 2048
WIDTH = 256
STRIPS = V // WIDTH
DEVICES = 128
ENTRIES = 96 * V * V
ORDERS = ("yzx", "xyz", "zxy", "yzx", "xyz", "zxy", "yzx", "xyz")
VT = V // TILE
GROUPS = ((0, 1, 2), (3, 4, 5), (6, 7))
MTILE = 1536
AHEAD = 2
STREAMS = ("one", "two", "ring", "relay", "side")


def place():
    row, col = lax.axis_index("row"), lax.axis_index("col")
    return {
        "x": row // 4,
        "zl": (row // 2) % 2,
        "c": row % 2,
        "zh": col // 4,
        "y": col % 4,
        "z": (col // 4) * 2 + (row // 2) % 2,
    }


def device(at):
    return {"row": at["x"] * 4 + (at["z"] % 2) * 2 + at["c"], "col": (at["z"] // 2) * 4 + at["y"]}


def block(gathered, strip, at, whole, half=None):
    every = slice(None)
    x, zl = (every if "x" in whole else at["x"]), (every if "z" in whole else at["zl"])
    if half is not None:
        if "x" in whole:
            x = pl.ds(2 * half, 2)
        else:
            zl = half
    return gathered.at[
        strip,
        x,
        zl,
        every if "z" in whole else at["zh"],
        at["c"],
        every if "y" in whole else at["y"],
    ]


def moved(at, axis, hops):
    there = dict(at)
    there[axis] = (at[axis] + hops) % 4
    if axis == "z":
        there["zl"], there["zh"] = there["z"] % 2, there["z"] // 2
    return there


def gather_kernel(
    lam_hbm, dress_hbm, const_hbm, mask_hbm, energy_hbm, shift_hbm,
    resid_ref, wide_ref, factor_ref,
    masked_ref, gathered, turned, const_ref, mask_ref, energy_ref, shift_ref, colmask, rowmask, squares, mine, everyone,
    small_sem, load_sem, own_sem, send_sem, recv_one, recv_two, recv_ring, recv_relay, recv_side, sum_send, sum_recv,
):
    at = place()
    col = lax.axis_index("col")
    other_core = dict(at, c=1 - at["c"])
    barrier = pltpu.get_barrier_semaphore()
    partners = [device(moved(at, axis, hops)) for axis in "xyz" for hops in (2, 1, 3)] + [device(other_core)]
    for partner in partners:
        pl.semaphore_signal(barrier, inc=1, device_id=partner, device_id_type=MESH)

    own = [
        pltpu.make_async_copy(dress_hbm.at[:, pl.ds(s * WIDTH, WIDTH)], block(gathered, s, at, ""), own_sem)
        for s in range(STRIPS)
    ]
    for copy in own:
        copy.start()
    small = [
        pltpu.make_async_copy(mask_hbm, mask_ref, small_sem.at[0]),
        pltpu.make_async_copy(energy_hbm, energy_ref, small_sem.at[1]),
        pltpu.make_async_copy(shift_hbm, shift_ref, small_sem.at[2]),
    ]
    for copy in small:
        copy.start()
    def load(p):
        rows = pl.ds(pl.multiple_of(p * ROWS, ROWS), ROWS)
        pltpu.make_async_copy(lam_hbm.at[p], masked_ref.at[rows, :], load_sem.at[0, p]).start()
        pltpu.make_async_copy(const_hbm.at[p], const_ref.at[rows, :], load_sem.at[1, p]).start()

    def wait_blocks(ref, sem):
        pltpu.make_async_copy(ref, ref, sem).wait()

    pl.semaphore_wait(barrier, len(partners))

    def send(part, target, stream, recv, source=None):
        pltpu.make_async_remote_copy(
            src_ref=part if source is None else source,
            dst_ref=part,
            send_sem=send_sem.at[STREAMS.index(stream)],
            recv_sem=recv,
            device_id=device(target),
            device_id_type=MESH,
        ).start()

    def spread_one(s):
        order = ORDERS[s]
        for hops in (2, 1, 3):
            source = dress_hbm.at[:, pl.ds(s * WIDTH, WIDTH)]
            send(block(gathered, s, at, ""), moved(at, order[0], hops), "one", recv_one, source)

    def spread_two(s):
        order = ORDERS[s]
        for hops in (2, 1, 3):
            send(block(gathered, s, at, order[0]), moved(at, order[1], hops), "two", recv_two.at[s])

    def spread_ring(s):
        order = ORDERS[s]
        for hops in (1, 3):
            send(block(gathered, s, at, order[:2]), moved(at, order[2], hops), "ring", recv_ring.at[s])
        send(block(gathered, s, at, order[:2]), other_core, "side", recv_side.at[0, s])

    def relay(s):
        order = ORDERS[s]
        wait_blocks(gathered.at[s, 0:2, :, :, 0, :], recv_ring.at[s])
        for hops, half in ((1, 0), (3, 1)):
            source = moved(at, order[2], -hops)
            send(block(gathered, s, source, order[:2], half), moved(at, order[2], hops), "relay", recv_relay.at[s])
        for hops in (1, 3):
            send(block(gathered, s, moved(at, order[2], hops), order[:2]), other_core, "side", recv_side.at[1, s])

    def land(s):
        order = ORDERS[s]
        wait_blocks(gathered.at[s, 0, :, :, 0, :], recv_relay.at[s])
        send(block(gathered, s, moved(at, order[2], 2), order[:2]), other_core, "side", recv_side.at[2, s])

    def ready(s):
        wait_blocks(gathered.at[s, 0, :, :, 0, :], recv_side.at[0, s])
        wait_blocks(gathered.at[s, 0:2, :, :, 0, :], recv_side.at[1, s])
        wait_blocks(gathered.at[s, 0, :, :, 0, :], recv_side.at[2, s])

    for s in range(STRIPS):
        spread_one(s)

    for copy in small:
        copy.wait()
    mask = mask_ref[...].astype(F32)
    tile_of = lax.broadcasted_iota(jnp.int32, (VT, V), 0)
    tile_col = lax.broadcasted_iota(jnp.int32, (VT, V), 1) // TILE
    cols_of = jnp.dot(mask, (tile_of == tile_col).astype(F32), preferred_element_type=F32)
    row_tile = lax.broadcasted_iota(jnp.int32, (ROWS, VT), 0) // TILE + col * (ROWS // TILE)
    row_hot = (row_tile == lax.broadcasted_iota(jnp.int32, (ROWS, VT), 1)).astype(F32)
    for p in range(PAIRS):
        colmask[p] = cols_of[p : p + 1, :]
        rowmask[p] = jnp.sum(row_hot * mask[p : p + 1, :], axis=1, keepdims=True)
    squares[...] = jnp.zeros_like(squares)

    wait_blocks(gathered.at[:, 0, 0, 0, 0, 0], own_sem)
    wait_blocks(gathered.at[:, 0:3, 0, 0, 0, 0], recv_one)
    for s in range(STRIPS):
        spread_two(s)

    def prepare(p, carry):
        rows = pl.ds(pl.multiple_of(p * ROWS, ROWS), ROWS)
        for ref, k in ((masked_ref, 0), (const_ref, 1)):
            pltpu.make_async_copy(ref.at[rows, :], ref.at[rows, :], load_sem.at[k, p]).wait()

        @pl.when(p + AHEAD < PAIRS)
        def _():
            load(p + AHEAD)

        for q in range(V // 256):
            cols = pl.ds(q * 256, 256)
            domain = (rowmask[p] * colmask[p, :, cols]).astype(BF16)
            part = masked_ref[rows, cols] * domain
            masked_ref[rows, cols] = part
            pieces = [part[:, k * 64 : (k + 1) * 64] for k in (0, 2, 1, 3)]
            turned[rows, cols] = jnp.concatenate(pieces, axis=1)
            const_ref[rows, cols] = const_ref[rows, cols] * domain
        return carry

    def arrive_two(s):
        wait_blocks(gathered.at[s, 0:3, 0, 0, 0, :], recv_two.at[s])
        spread_ring(s)

    for s in GROUPS[0]:
        arrive_two(s)
    for p in range(AHEAD):
        load(p)
    for s in GROUPS[1]:
        arrive_two(s)
    lax.fori_loop(0, PAIRS, prepare, 0)

    def plane_product(s, axis, hops):
        there = moved(at, axis, hops)
        if axis == "x":
            left = turned[:, pl.ds(pl.multiple_of(there["x"] * 512, 512), 512)]
            right = gathered[s, there["x"]]
        else:
            offset = there["zl"] * 256 + there["zh"] * 128
            pieces = [turned[:, pl.ds(pl.multiple_of(x * 512 + offset, 128), 128)] for x in range(4)]
            left = jnp.concatenate(pieces, axis=1)
            right = gathered[s, :, there["zl"], there["zh"]]
        return jnp.dot(left, right.reshape(512, WIDTH), preferred_element_type=F32)

    def near(s, axis):
        cols = pl.ds(s * WIDTH, WIDTH)
        wait_blocks(gathered.at[s, 0, :, :, 0, :], recv_side.at[0, s])
        resid_ref[:, cols] = const_ref[:, cols].astype(F32) + plane_product(s, axis, 0)

    def beside(s, axis):
        cols = pl.ds(s * WIDTH, WIDTH)
        wait_blocks(gathered.at[s, 0:2, :, :, 0, :], recv_side.at[1, s])

        def add(k, carry):
            resid_ref[:, cols] += plane_product(s, axis, 2 * k + 1)
            return carry

        lax.fori_loop(0, 2, add, 0)

    def far(s, axis):
        cols = pl.ds(s * WIDTH, WIDTH)
        wait_blocks(gathered.at[s, 0, :, :, 0, :], recv_side.at[2, s])
        product = plane_product(s, axis, 2)
        total = jnp.zeros((8, WIDTH), F32)
        for p in range(PAIRS):
            rows = pl.ds(p * ROWS, ROWS)
            part = colmask[p, :, cols] * (resid_ref[rows, cols] + product[p * ROWS : (p + 1) * ROWS, :])
            resid_ref[rows, cols] = part
            total = total + jnp.sum((part * part).reshape(ROWS // 8, 8, WIDTH), axis=0)
        squares[...] += total

    for s in GROUPS[0]:
        relay(s)
    for s in GROUPS[2]:
        arrive_two(s)
    near(0, "x")
    near(1, "z")
    for s in GROUPS[1]:
        relay(s)
    beside(0, "x")
    beside(1, "z")
    for s in GROUPS[0]:
        land(s)
    far(0, "x")
    far(1, "z")

    def strip(s, carry):
        @pl.when(s == 2)
        def _():
            for later in GROUPS[2]:
                relay(later)
            for later in GROUPS[1]:
                land(later)

        @pl.when(s == 4)
        def _():
            for later in GROUPS[2]:
                land(later)

        ready(s)
        cols = pl.ds(pl.multiple_of(s * WIDTH, WIDTH), WIDTH)

        def rows_of(i, carry):
            rows = pl.ds(pl.multiple_of(i * MTILE, MTILE), MTILE)
            product = jnp.dot(turned[rows, :], gathered[s].reshape(V, WIDTH), preferred_element_type=F32)
            total = jnp.zeros((8, WIDTH), F32)
            for q in range(MTILE // ROWS):
                p = i * (MTILE // ROWS) + q
                pair_rows = pl.ds(pl.multiple_of(p * ROWS, ROWS), ROWS)
                part = const_ref[pair_rows, cols].astype(F32) + colmask[p, :, cols] * product[q * ROWS : (q + 1) * ROWS, :]
                resid_ref[pair_rows, cols] = part
                total = total + jnp.sum((part * part).reshape(ROWS // 8, 8, WIDTH), axis=0)
            squares[...] += total
            return carry

        lax.fori_loop(0, PAIRS * ROWS // MTILE, rows_of, 0)
        return carry

    lax.fori_loop(2, STRIPS, strip, 0)

    eight = squares[:, :128] + squares[:, 128:]
    mine[...] = jnp.sum(eight, axis=0, keepdims=True)
    me = lax.axis_index("row") * 8 + col

    offsets = [(dx, dy, dz, dc) for dx in range(4) for dy in range(4) for dz in range(4) for dc in range(2)][1:]
    offsets.sort(key=lambda o: (-sum(min(d, 4 - d) for d in o[:3]), o))
    xs, ys, zs = ([(at[a] + d) % 4 for d in range(4)] for a in "xyz")
    row_parts = [[x * 4 + (z % 2) * 2 for z in zs] for x in xs]
    col_parts = [[(z // 2) * 4 + y for z in zs] for y in ys]
    for dx, dy, dz, dc in offsets:
        core = at["c"] if dc == 0 else other_core["c"]
        pltpu.make_async_remote_copy(
            src_ref=mine,
            dst_ref=everyone.at[me],
            send_sem=sum_send,
            recv_sem=sum_recv,
            device_id={"row": row_parts[dx][dz] + core, "col": col_parts[dy][dz]},
            device_id_type=MESH,
        ).start()
    everyone[me] = mine[...]

    own_energy = energy_ref[:, pl.ds(pl.multiple_of(col * ROWS, ROWS), ROWS)]
    diagonal = lax.broadcasted_iota(jnp.int32, (ROWS, ROWS), 0) == lax.broadcasted_iota(jnp.int32, (ROWS, ROWS), 1)
    energy_rows = jnp.sum(jnp.where(diagonal, own_energy, 0.0), axis=1, keepdims=True)

    def divide(p, carry):
        shifted = energy_rows + shift_ref[p]
        for s in range(STRIPS):
            rows, cols = pl.ds(pl.multiple_of(p * ROWS, ROWS), ROWS), pl.ds(s * WIDTH, WIDTH)
            resid_ref[rows, cols] = resid_ref[rows, cols] / (shifted + energy_ref[:, cols])
        return carry

    lax.fori_loop(0, PAIRS, divide, 0)

    def widen(p, carry):
        rows = pl.ds(pl.multiple_of(p * ROWS, ROWS), ROWS)
        wide_ref[rows, :] = masked_ref[rows, :].astype(F32)
        return carry

    lax.fori_loop(0, PAIRS, widen, 0)

    wait_blocks(everyone.at[0 : DEVICES - 1], sum_recv)
    total = jnp.sum(jnp.sum(everyone[...], axis=0), axis=1, keepdims=True)
    factor = 0.25 * lax.rsqrt(total / ENTRIES + 1e-06)
    factor_ref[...] = jnp.zeros((8, 128), F32) + factor

    wait_blocks(gathered.at[:, 0:3, 0, 0, 0, 0], send_sem.at[0])
    wait_blocks(gathered.at[:, 0:3, 0, 0, 0, :], send_sem.at[1])
    wait_blocks(gathered.at[:, :, :, :, 0, 0:2], send_sem.at[2])
    wait_blocks(gathered.at[:, :, :, :, 0, 0], send_sem.at[3])
    wait_blocks(gathered.at[:, :, :, :, 0, :], send_sem.at[4])
    wait_blocks(everyone.at[0 : DEVICES - 1], sum_send)


CHUNK = 64


def update_kernel(resid_ref, masked_ref, factor_ref, out_hbm, staged, sem):
    factor = factor_ref[0:1, 0:1]
    copies = []
    for i in range(PAIRS * ROWS // CHUNK):
        rows = pl.ds(i * CHUNK, CHUNK)
        staged[rows, :] = (masked_ref[rows, :] + factor * resid_ref[rows, :]).astype(BF16)
        copies.append(pltpu.make_async_copy(staged.at[rows, :], out_hbm.at[rows, :], sem.at[i]))
        copies[-1].start()
    for copy in copies:
        copy.wait()


def per_device(lambda_tiles, dressing, constant_term, domain_mask, virtual_energy, pair_shift):
    vmem, hbm = (pl.BlockSpec(memory_space=m) for m in (pltpu.VMEM, pl.ANY))
    flat = (PAIRS * ROWS, V)
    dma = pltpu.SemaphoreType.DMA
    resid, masked, factor = pl.pallas_call(
        gather_kernel,
        name="gather_multiply",
        out_shape=(pltpu.VMEM(flat, F32), pltpu.VMEM(flat, F32), pltpu.VMEM((8, 128), F32)),
        in_specs=[hbm] * 6,
        out_specs=(vmem, vmem, vmem),
        scratch_shapes=[
            pltpu.VMEM(flat, BF16),
            pltpu.VMEM((STRIPS, 4, 2, 2, 2, 4, 16, WIDTH), BF16),
            pltpu.VMEM(flat, BF16),
            pltpu.VMEM(flat, BF16),
            pltpu.VMEM((PAIRS, VT), jnp.int32),
            pltpu.VMEM((1, V), F32),
            pltpu.SMEM((PAIRS,), F32),
            pltpu.VMEM((PAIRS, 1, V), F32),
            pltpu.VMEM((PAIRS, ROWS, 1), F32),
            pltpu.VMEM((8, WIDTH), F32),
            pltpu.VMEM((1, 128), F32),
            pltpu.VMEM((DEVICES, 1, 128), F32),
            dma((3,)),
            dma((2, PAIRS)),
            dma,
            dma((len(STREAMS),)),
            dma,
            dma((STRIPS,)),
            dma((STRIPS,)),
            dma((STRIPS,)),
            dma((3, STRIPS)),
            dma,
            dma,
        ],
        compiler_params=pltpu.CompilerParams(
            collective_id=0, has_side_effects=True, vmem_limit_bytes=36 << 20
        ),
    )(lambda_tiles, dressing, constant_term, domain_mask, virtual_energy.reshape(1, V), pair_shift)
    resid = pltpu.with_memory_space_constraint(resid, pltpu.VMEM)
    masked = pltpu.with_memory_space_constraint(masked, pltpu.VMEM)
    out = pl.pallas_call(
        update_kernel,
        name="scale_update",
        out_shape=jax.ShapeDtypeStruct(flat, BF16),
        in_specs=[vmem, vmem, vmem],
        out_specs=hbm,
        scratch_shapes=[pltpu.VMEM(flat, BF16), dma((PAIRS * ROWS // CHUNK,))],
        compiler_params=pltpu.CompilerParams(vmem_limit_bytes=8 << 20),
    )(resid, masked, factor)
    return out.reshape(PAIRS, ROWS, V)


def solution(mesh):
    return jax.shard_map(
        per_device,
        mesh=mesh,
        in_specs=(
            P("row", "col", None),
            P(("row", "col"), None),
            P("row", "col", None),
            P("row", None),
            P(),
            P("row"),
        ),
        out_specs=P("row", "col", None),
        check_vma=False,
    )
```
